32 devices in a mesh: seq: 8 (over z, x), ch: 4 (over y, core).
Axes of the slice: x: 2, y: 2, z: 4, core: 2. Of those that a mesh axis runs over, the one named last changes fastest.
Arguments:
- sequence: bfloat16 [4096, 4096], P('seq', 'ch'), may hold values from -6 to 6
- in_weight: bfloat16 [4096, 3, 4096], P(None, None, 'ch'), may hold values from -0.09375 to 0.09375
- short_weight: bfloat16 [7, 3, 4096], P(None, None, 'ch'), may hold values from -2.5 to 2.5
- filter_taps: bfloat16 [4096, 4096], P('seq', 'ch'), may hold values from -1 to 1
- out_weight: bfloat16 [4096, 4096], P('ch'), may hold values from -0.09375 to 0.09375
Outputs:
- result: bfloat16 [4096, 4096], P('seq', 'ch')
The draws below stay inside these ranges and needn't reach their ends.
All inputs are finite; a program needn't handle non-finite values.
Results may differ from the reference program's by a relative error of at most 0.014.
Values may be sent and summed in bfloat16 or wider, within the bound.
No kernel may reach another device: no remote copies, remote signals or barrier semaphores. Data moves between devices by JAX's collectives and lax.ppermute only.
A program may use at most 192 MiB of HBM per device.

```python
import jax
import jax.numpy as jnp
from jax import lax

D = 4096
TAPS = 7
SEQUENCE_LENGTH = 4096


def draw_filter_taps(key, part):
    key_rate = jax.random.fold_in(key, 11)
    key_noise = jax.random.fold_in(key, 12)
    pulse_random_key = jax.random.fold_in(key, 13)
    position_indices = jnp.arange(SEQUENCE_LENGTH).astype(jnp.float32)[:, None]
    low = jnp.log(0.5 / SEQUENCE_LENGTH)
    high = jnp.log(1.0 / 30.0)
    rates = jnp.exp(jax.random.uniform(key_rate, (1, D), jnp.float32, low, high))
    noise = jax.random.truncated_normal(key_noise, -3.0, 3.0, (SEQUENCE_LENGTH, D), jnp.float32)
    noise_pulses = jax.random.randint(pulse_random_key, (3,), 0, SEQUENCE_LENGTH).astype(jnp.float32)
    dropout_flags = jnp.prod(jnp.where(position_indices[:, :, None] >= noise_pulses[None, None, :], 0.6, 1.0), axis=2)
    amplitude = jnp.sqrt(2.0 * rates)
    return (amplitude * jnp.exp(-rates * position_indices) * dropout_flags * noise).astype(jnp.bfloat16)


def shard_levels(key, extent, pieces, smallest, largest):
    def one(dim, shards_of):
        heights = jax.random.uniform(jax.random.fold_in(jax.random.fold_in(key, 6), dim), (shards_of,), jnp.float32, smallest / len(pieces), largest / len(pieces))
        return jnp.repeat(jnp.exp(heights), extent[dim] // shards_of).reshape((-1,) + (1,) * (len(extent) - dim - 1))

    factor_of = one(*pieces[0])
    for cut in pieces[1:]:
        factor_of = factor_of * one(*cut)
    return factor_of


def bell_draw(own_key, shape, spread, limit, pieces=(), kind=jnp.bfloat16):
    factor_of = shard_levels(own_key, shape, pieces, -0.22, 0.18) if pieces else 1.0
    values = jax.random.normal(own_key, shape, jnp.float32) * spread * factor_of
    return jnp.minimum(jnp.maximum(values, -limit), limit).astype(kind)


def setup_inputs(seed: int = 0) -> dict:
    key_of = jax.random.split(jax.random.key(seed), 6)
    sequence = bell_draw(key_of[0], (SEQUENCE_LENGTH, D), 1.0, 6.0, ((0, 8), (1, 4)))
    in_weight = bell_draw(key_of[1], (D, 3, D), D ** -0.5, 0.09375, ((2, 4),))
    short_weight = bell_draw(key_of[2], (TAPS, 3, D), 0.4, 2.5, ((2, 4),))
    filter_taps = draw_filter_taps(jax.random.fold_in(key_of[5], 71), 0)
    out_weight = bell_draw(key_of[4], (D, D), D ** -0.5, 0.09375, ((0, 4),))
    return dict(sequence=sequence, in_weight=in_weight, short_weight=short_weight, filter_taps=filter_taps, out_weight=out_weight)


def convolve_block(operands):
    signal, taps_block = operands
    length = signal.shape[0]
    padded_len = 2 * length
    spectrum = jnp.fft.rfft(signal.astype(jnp.float32), n=padded_len, axis=0) * jnp.fft.rfft(taps_block.astype(jnp.float32), n=padded_len, axis=0)
    return jnp.fft.irfft(spectrum, n=padded_len, axis=0)[:length].astype(jnp.float32)


def reference(sequence, in_weight, short_weight, filter_taps, out_weight):
    length = sequence.shape[0]
    mixed_parts = []
    for branch in range(3):
        projected = jnp.dot(sequence, in_weight[:, branch, :], preferred_element_type=jnp.float32).astype(jnp.bfloat16)
        zero_extended = jnp.pad(projected.astype(jnp.float32), ((TAPS - 1, 0), (0, 0)))
        running = jnp.zeros((length, D), jnp.float32)
        for offset in range(TAPS):
            lead = TAPS - 1 - offset
            running = running + short_weight[offset, branch].astype(jnp.float32) * zero_extended[lead:lead + length]
        mixed_parts.append(running.astype(jnp.bfloat16))
    query, keys_part, values_part = mixed_parts
    product = (keys_part.astype(jnp.float32) * values_part.astype(jnp.float32)).astype(jnp.bfloat16)
    block_count = D // 128

    def to_blocks(array):
        return array.reshape(length, block_count, 128).transpose(1, 0, 2)

    convolved = lax.map(convolve_block, (to_blocks(product), to_blocks(filter_taps)))
    convolved = convolved.transpose(1, 0, 2).reshape(length, D)
    gated = (query.astype(jnp.float32) * convolved).astype(jnp.bfloat16)
    return jnp.dot(gated, out_weight, preferred_element_type=jnp.float32).astype(jnp.bfloat16)
```

```python
import math

import jax
import jax.numpy as jnp
import numpy as np
from jax import lax
from jax.experimental import pallas as pl
from jax.experimental.pallas import tpu as pltpu
from jax.sharding import PartitionSpec as P

TAPS = 7
HALO = 16
bf16 = jnp.bfloat16
f32 = jnp.float32


def split_parts(table):
    high = table.astype(bf16)
    low = (table - high.astype(np.float64)).astype(bf16)
    return high, low


def fourier_tables(block):
    freqs = np.arange(block)[:, None] + 0.5
    spots = np.arange(block)[None, :]
    angle = 2.0 * math.pi * freqs * spots / (2 * block)
    forward = np.concatenate([np.cos(angle), -np.sin(angle)], 0)
    backward = np.concatenate([np.cos(angle).T, -np.sin(angle).T], 1) / block
    fwd_high, fwd_low = split_parts(forward)
    bwd_high, bwd_low = split_parts(backward)
    fwd = np.concatenate([fwd_high, fwd_low], 1)
    bwd = np.concatenate([bwd_high, bwd_low, bwd_high], 1)
    sign = np.broadcast_to(np.where(np.arange(8) % 2 == 0, 1.0, -1.0)[:, None], (8, 128))
    return fwd, bwd, sign.astype(np.float32)


def swap(shard, axis, bit):
    size = lax.axis_size(axis)
    return lax.ppermute(shard, axis, [(i, i ^ bit) for i in range(size)])


def vmem_spec():
    return pl.BlockSpec(memory_space=pltpu.VMEM)


def params(mib):
    return pltpu.CompilerParams(vmem_limit_bytes=mib * 1024 * 1024)


def cost(flops, moved):
    return pl.CostEstimate(flops=flops, bytes_accessed=moved, transcendentals=0)


def project_kernel(pieces, strip, own_ref, *refs):
    x_refs = refs[:pieces]
    w_refs = refs[pieces : 2 * pieces]
    tap_ref, query_ref, product_ref, ext_ref = refs[2 * pieces :]
    rows, width = query_ref.shape
    for branch in range(3):
        total = None
        for x_ref, w_ref in zip(x_refs, w_refs):
            term = jnp.dot(x_ref[...], w_ref[branch], preferred_element_type=f32)
            total = term if total is None else total + term
        ext_ref[branch] = total.astype(bf16).astype(f32)
    step = 64
    for lane in range(0, width, strip):
        lanes = slice(lane, lane + strip)
        for row in range(0, rows, step):

            def mixed(branch):
                running = None
                for offset in range(TAPS):
                    lead = row + HALO - offset
                    term = tap_ref[branch, offset : offset + 1, lanes] * ext_ref[branch, lead : lead + step, lanes]
                    running = term if running is None else running + term
                return running.astype(bf16)

            here = slice(row, row + step)
            query_ref[here, lanes] = mixed(0)
            product = (mixed(1).astype(f32) * mixed(2).astype(f32)).astype(bf16)
            if len(product_ref.shape) == 3:
                product_ref[lane // strip, here, :] = product
            else:
                product_ref[here, lanes] = product


def project(own, pieces, weights, tap_table, blocks):
    count = len(pieces)
    rows_in, depth = pieces[0].shape
    rows = rows_in - HALO
    width = weights.shape[2]
    tile = 256
    chan = width // blocks
    direct = chan % 128 == 0 and tile % chan == 0
    strip = chan if direct else 128
    if direct:
        product_shape = (blocks, rows, chan)
        product_spec = pl.BlockSpec((tile // chan, rows, chan), lambda i, own: (i, 0, 0))
    else:
        product_shape = (rows, width)
        product_spec = pl.BlockSpec((rows, tile), lambda i, own: (0, i))

    def weight_spec(p):
        return pl.BlockSpec((3, depth, tile), lambda i, own: (0, own[0] ^ p, i))

    query, product = pl.pallas_call(
        lambda *refs: project_kernel(count, strip, *refs),
        grid_spec=pltpu.PrefetchScalarGridSpec(
            num_scalar_prefetch=1,
            grid=(width // tile,),
            in_specs=[vmem_spec()] * count
            + [weight_spec(p) for p in range(count)]
            + [pl.BlockSpec((3, TAPS, tile), lambda i, own: (0, 0, i))],
            out_specs=[pl.BlockSpec((rows, tile), lambda i, own: (0, i)), product_spec],
            scratch_shapes=[pltpu.VMEM((3, rows_in, tile), f32)],
        ),
        out_shape=[
            jax.ShapeDtypeStruct((rows, width), bf16),
            jax.ShapeDtypeStruct(product_shape, bf16),
        ],
        compiler_params=params(32),
        cost_estimate=cost(2 * rows_in * count * depth * 3 * width, 6 * count * depth * width),
        name="project",
    )(own, *pieces, *([weights] * count), tap_table)
    if not direct:
        product = product.reshape(rows, blocks, chan).transpose(1, 0, 2)
    return query, product


def transform_into(fwd_ref, in_ref, picks, out_ref, places):
    block, chan = in_ref.shape[1:]
    group = 2 if chan % 128 == 0 and len(picks) % 2 == 0 else 1
    for start in range(0, len(picks), group):
        signal = jnp.concatenate([in_ref[k] for k in picks[start : start + group]], 1)
        stacked = jnp.concatenate([signal, signal], 0)
        result = jnp.dot(fwd_ref[...], stacked, preferred_element_type=f32)
        for j in range(group):
            lanes = slice(j * chan, (j + 1) * chan)
            out_ref[0, places[start + j]] = result[:block, lanes]
            out_ref[1, places[start + j]] = result[block:, lanes]


def filter_kernel(fwd_ref, sign_ref, taps_ref, out_ref, spec_ref):
    count, block, chan = taps_ref.shape
    transform_into(fwd_ref, taps_ref, range(count), spec_ref, range(count))
    sign = sign_ref[:, :chan]

    def body(i, carry):
        rows = pl.ds(pl.multiple_of(i * 8, 8), 8)
        prev = None
        for k in range(count):
            real, imag = spec_ref[0, k, rows, :], spec_ref[1, k, rows, :]
            if prev is None:
                out_ref[0, k, rows, :] = real
                out_ref[1, k, rows, :] = imag
            else:
                out_ref[0, k, rows, :] = real - sign * prev[1]
                out_ref[1, k, rows, :] = imag + sign * prev[0]
            prev = (real, imag)
        return carry

    lax.fori_loop(0, block // 8, body, 0)


def filter_spectra(fwd, sign, taps):
    count, block, chan = taps.shape
    shape = (2, count, block, chan)
    return pl.pallas_call(
        filter_kernel,
        in_specs=[vmem_spec()] * 3,
        out_specs=vmem_spec(),
        out_shape=jax.ShapeDtypeStruct(shape, f32),
        scratch_shapes=[pltpu.VMEM(shape, f32)],
        compiler_params=params(32),
        cost_estimate=cost(2 * 2 * count * chan * 4 * block * block, 8 * count * block * chan),
        name="filter_spectra",
    )(fwd, sign, taps)


def accumulate(filt_ref, spec_ref, sources, init_ref, targets, write):
    block = filt_ref.shape[2]

    def body(i, carry):
        rows = pl.ds(pl.multiple_of(i * 8, 8), 8)
        for place, target in enumerate(targets):
            real = imag = None
            if init_ref is not None:
                real, imag = init_ref[0, place, rows, :], init_ref[1, place, rows, :]
            for slot, source in enumerate(sources):
                if source > target:
                    continue
                lag = target - source
                xr, xi = spec_ref[0, slot, rows, :], spec_ref[1, slot, rows, :]
                gr, gi = filt_ref[0, lag, rows, :], filt_ref[1, lag, rows, :]
                if real is None:
                    real, imag = xr * gr - xi * gi, xr * gi + xi * gr
                else:
                    real = real + xr * gr - xi * gi
                    imag = imag + xr * gi + xi * gr
            if real is None:
                real = imag = jnp.zeros((8, filt_ref.shape[3]), f32)
            write(rows, place, real, imag)
        return carry

    lax.fori_loop(0, block // 8, body, 0)


def inverse_into(bwd_ref, sum_ref, out_ref):
    count, double, chan = sum_ref.shape
    group = 2 if chan % 128 == 0 and count % 2 == 0 else 1
    for start in range(0, count, group):
        full = jnp.concatenate([sum_ref[start + j] for j in range(group)], 1)
        high = full.astype(bf16)
        low = (full - high.astype(f32)).astype(bf16)
        stacked = jnp.concatenate([high, high, low], 0)
        result = jnp.dot(bwd_ref[...], stacked, preferred_element_type=f32).astype(out_ref.dtype)
        for j in range(group):
            out_ref[start + j] = result[:, j * chan : (j + 1) * chan]


def early_kernel(fwd_ref, filt_ref, half_ref, same_ref, other_ref, spec_ref):
    half = half_ref.shape[0]
    odd, even = [2 * k + 1 for k in range(half)], [2 * k for k in range(half)]
    transform_into(fwd_ref, half_ref, range(half), spec_ref, range(half))

    def to(ref):
        def write(rows, place, real, imag):
            ref[0, place, rows, :] = real
            ref[1, place, rows, :] = imag

        return write

    accumulate(filt_ref, spec_ref, odd, None, odd, to(same_ref))
    accumulate(filt_ref, spec_ref, odd, None, even, to(other_ref))


def write_sums(sum_ref, block):
    def write(rows, place, real, imag):
        sum_ref[place, rows, :] = real
        sum_ref[place, pl.ds(rows.start + block, 8), :] = imag

    return write


def middle_kernel(fwd_ref, bwd_ref, filt_ref, half_ref, init_ref, out_ref, spec_ref, sum_ref):
    half, block, _ = half_ref.shape
    even = [2 * k for k in range(half)]
    transform_into(fwd_ref, half_ref, range(half), spec_ref, range(half))
    accumulate(filt_ref, spec_ref, even, init_ref, even, write_sums(sum_ref, block))
    inverse_into(bwd_ref, sum_ref, out_ref)


def late_kernel(bwd_ref, filt_ref, spec_ref, init_ref, out_ref, sum_ref):
    _, half, block, _ = spec_ref.shape
    odd, even = [2 * k + 1 for k in range(half)], [2 * k for k in range(half)]
    accumulate(filt_ref, spec_ref, even, init_ref, odd, write_sums(sum_ref, block))
    inverse_into(bwd_ref, sum_ref, out_ref)


def early(fwd, filt, part):
    half, block, chan = part.shape
    spec = jax.ShapeDtypeStruct((2, half, block, chan), f32)
    return pl.pallas_call(
        early_kernel,
        in_specs=[vmem_spec()] * 3,
        out_specs=[vmem_spec()] * 2,
        out_shape=[spec, spec],
        scratch_shapes=[pltpu.VMEM(spec.shape, f32)],
        compiler_params=params(32),
        cost_estimate=cost(2 * half * chan * 4 * block * block * 2, 32 * half * block * chan),
        name="early_blocks",
    )(fwd, filt, part)


def middle(fwd, bwd, filt, part, init):
    half, block, chan = part.shape
    spec = jax.ShapeDtypeStruct((2, half, block, chan), f32)
    return pl.pallas_call(
        middle_kernel,
        in_specs=[vmem_spec()] * 5,
        out_specs=[vmem_spec()] * 2,
        out_shape=[jax.ShapeDtypeStruct(part.shape, bf16), spec],
        scratch_shapes=[pltpu.VMEM((half, 2 * block, chan), f32)],
        compiler_params=params(32),
        cost_estimate=cost(2 * half * chan * 10 * block * block * 2, 32 * half * block * chan),
        name="middle_blocks",
    )(fwd, bwd, filt, part, init)


def late(bwd, filt, spec, init):
    _, half, block, chan = spec.shape
    return pl.pallas_call(
        late_kernel,
        in_specs=[vmem_spec()] * 4,
        out_specs=vmem_spec(),
        out_shape=jax.ShapeDtypeStruct((half, block, chan), bf16),
        scratch_shapes=[pltpu.VMEM((half, 2 * block, chan), f32)],
        compiler_params=params(32),
        cost_estimate=cost(2 * half * chan * 6 * block * block * 2, 32 * half * block * chan),
        name="late_blocks",
    )(bwd, filt, spec, init)


def output_kernel(own_ref, query_ref, conv_ref, w_ref, out_ref, gated_ref):
    blocks, _, chan = conv_ref.shape

    @pl.when((pl.program_id(0) == 0) & (pl.program_id(1) == 0))
    def _():
        for k in range(blocks):
            lanes = slice(k * chan, (k + 1) * chan)
            gated_ref[:, lanes] = (query_ref[:, lanes].astype(f32) * conv_ref[k].astype(f32)).astype(bf16)

    out_ref[0] = jnp.dot(gated_ref[...], w_ref[...], preferred_element_type=f32).astype(bf16)


def output_terms(own, query, conv, weights, parts):
    rows, width = query.shape
    wide = weights.shape[1] // parts
    tile = 512
    tiles = wide // tile
    return pl.pallas_call(
        output_kernel,
        grid_spec=pltpu.PrefetchScalarGridSpec(
            num_scalar_prefetch=1,
            grid=(parts, tiles),
            in_specs=[
                vmem_spec(),
                vmem_spec(),
                pl.BlockSpec((width, tile), lambda p, i, own: (0, (own[0] ^ p) * tiles + i)),
            ],
            out_specs=pl.BlockSpec((1, rows, tile), lambda p, i, own: (p, 0, i)),
            scratch_shapes=[pltpu.VMEM((rows, width), bf16)],
        ),
        out_shape=jax.ShapeDtypeStruct((parts, rows, wide), bf16),
        compiler_params=params(24),
        cost_estimate=cost(2 * rows * width * parts * wide, 2 * width * parts * wide),
        name="output_terms",
    )(own, query, conv, weights)


def body(sequence, in_weight, short_weight, filter_taps, out_weight):
    rows, width = sequence.shape
    blocks = lax.axis_size("seq")
    parts = lax.axis_size("ch")
    chan = width // blocks
    block = rows // 2
    fwd, bwd, sign = fourier_tables(block)
    own = lax.axis_index("ch").astype(jnp.int32).reshape(1)
    weights = in_weight.transpose(1, 0, 2)
    tap_table = short_weight.astype(f32).transpose(1, 0, 2)
    bits = [1 << k for k in range(parts.bit_length() - 1)]

    def exchange(values):
        return lax.all_to_all(values, "seq", split_axis=0, concat_axis=0, tiled=True)

    taps = exchange(filter_taps.reshape(rows, blocks, chan).transpose(1, 0, 2))
    border = lax.ppermute(sequence[rows - HALO :], "seq", [(i, i + 1) for i in range(blocks - 1)])
    late_rows = sequence[block - HALO :]
    early_rows = jnp.concatenate([border, sequence[:block]], 0)

    def gather(shard):
        pieces = {0: shard}
        for bit in bits[1:] + bits[:1]:
            pieces.update({p | bit: swap(piece, "ch", bit) for p, piece in pieces.items()})
        return [pieces[p] for p in range(parts)]

    filt = filter_spectra(fwd, sign, taps.reshape(2 * blocks, block, chan))
    query_odd, product_odd = project(own, gather(late_rows), weights, tap_table, blocks)
    product_odd = exchange(product_odd)
    query_even, product_even = project(own, gather(early_rows), weights, tap_table, blocks)
    product_even = exchange(product_even)
    init_odd, init_even = early(fwd, filt, product_odd)
    conv_even, spec_even = middle(fwd, bwd, filt, product_even, init_even)
    conv_even = exchange(conv_even)
    conv_odd = late(bwd, filt, spec_even, init_odd)
    conv_odd = exchange(conv_odd)

    def finish(query, conv):
        terms = output_terms(own, query, conv, out_weight, parts)
        held = {p: terms[p] for p in range(parts)}
        for bit in bits:
            arrived = {p ^ bit: swap(held[p], "ch", bit) for p in held if p & bit}
            held = {p: (held[p].astype(f32) + arrived[p].astype(f32)).astype(bf16) for p in arrived}
        return held[0]

    return jnp.concatenate([finish(query_even, conv_even), finish(query_odd, conv_odd)], 0)


def solution(mesh):
    return jax.shard_map(
        body,
        mesh=mesh,
        in_specs=(
            P("seq", "ch"),
            P(None, None, "ch"),
            P(None, None, "ch"),
            P("seq", "ch"),
            P("ch", None),
        ),
        out_specs=P("seq", "ch"),
        check_vma=False,
    )
```

```python
import math

import jax
import jax.numpy as jnp
import numpy as np
from jax import lax
from jax.experimental import pallas as pl
from jax.experimental.pallas import tpu as pltpu
from jax.sharding import PartitionSpec as P

TAPS = 7
HALO = 16
bf16 = jnp.bfloat16
f32 = jnp.float32


def split_parts(table):
    high = table.astype(bf16)
    low = (table - high.astype(np.float64)).astype(bf16)
    return high, low


def fourier_tables(block):
    freqs = np.arange(block)[:, None] + 0.5
    spots = np.arange(block)[None, :]
    angle = 2.0 * math.pi * freqs * spots / (2 * block)
    forward = np.concatenate([np.cos(angle), -np.sin(angle)], 0)
    backward = np.concatenate([np.cos(angle).T, -np.sin(angle).T], 1) / block
    fwd_high, fwd_low = split_parts(forward)
    bwd_high, bwd_low = split_parts(backward)
    fwd = np.concatenate([fwd_high, fwd_low], 1)
    bwd = np.concatenate([bwd_high, bwd_low, bwd_high], 1)
    sign = np.broadcast_to(np.where(np.arange(8) % 2 == 0, 1.0, -1.0)[:, None], (8, 128))
    return fwd, bwd, sign.astype(np.float32)


def swap(shard, axis, bit):
    size = lax.axis_size(axis)
    return lax.ppermute(shard, axis, [(i, i ^ bit) for i in range(size)])


def vmem_spec():
    return pl.BlockSpec(memory_space=pltpu.VMEM)


def hbm_spec():
    return pl.BlockSpec(memory_space=pltpu.HBM)


def pinned(array):
    return pltpu.with_memory_space_constraint(array, pltpu.HBM)


def params(mib):
    return pltpu.CompilerParams(vmem_limit_bytes=mib * 1024 * 1024)


def cost(flops, moved):
    return pl.CostEstimate(flops=flops, bytes_accessed=moved, transcendentals=0)


def project_kernel(pieces, strip, own_ref, *refs):
    x_refs = refs[:pieces]
    w_refs = refs[pieces : 2 * pieces]
    tap_ref, query_ref, product_ref, ext_ref = refs[2 * pieces :]
    rows, width = query_ref.shape
    for branch in range(3):
        total = None
        for x_ref, w_ref in zip(x_refs, w_refs):
            term = jnp.dot(x_ref[...], w_ref[branch], preferred_element_type=f32)
            total = term if total is None else total + term
        ext_ref[branch] = total.astype(bf16).astype(f32)
    step = 64
    for lane in range(0, width, strip):
        lanes = slice(lane, lane + strip)
        for row in range(0, rows, step):

            def mixed(branch):
                running = None
                for offset in range(TAPS):
                    lead = row + HALO - offset
                    term = tap_ref[branch, offset : offset + 1, lanes] * ext_ref[branch, lead : lead + step, lanes]
                    running = term if running is None else running + term
                return running.astype(bf16)

            here = slice(row, row + step)
            query_ref[here, lanes] = mixed(0)
            product = (mixed(1).astype(f32) * mixed(2).astype(f32)).astype(bf16)
            if len(product_ref.shape) == 3:
                product_ref[lane // strip, here, :] = product
            else:
                product_ref[here, lanes] = product


def project(own, pieces, weights, tap_table, blocks):
    count = len(pieces)
    rows_in, depth = pieces[0].shape
    rows = rows_in - HALO
    width = weights.shape[2]
    tile = 256
    chan = width // blocks
    direct = chan % 128 == 0 and tile % chan == 0
    strip = chan if direct else 128
    if direct:
        product_shape = (blocks, rows, chan)
        product_spec = pl.BlockSpec((tile // chan, rows, chan), lambda i, own: (i, 0, 0))
    else:
        product_shape = (rows, width)
        product_spec = pl.BlockSpec((rows, tile), lambda i, own: (0, i))

    def weight_spec(p):
        return pl.BlockSpec((3, depth, tile), lambda i, own: (0, own[0] ^ p, i))

    query, product = pl.pallas_call(
        lambda *refs: project_kernel(count, strip, *refs),
        grid_spec=pltpu.PrefetchScalarGridSpec(
            num_scalar_prefetch=1,
            grid=(width // tile,),
            in_specs=[vmem_spec()] * count
            + [weight_spec(p) for p in range(count)]
            + [pl.BlockSpec((3, TAPS, tile), lambda i, own: (0, 0, i))],
            out_specs=[pl.BlockSpec((rows, tile), lambda i, own: (0, i)), product_spec],
            scratch_shapes=[pltpu.VMEM((3, rows_in, tile), f32)],
        ),
        out_shape=[pltpu.HBM((rows, width), bf16), pltpu.HBM(product_shape, bf16)],
        compiler_params=params(20),
        cost_estimate=cost(2 * rows_in * count * depth * 3 * width, 6 * count * depth * width),
        name="project",
    )(own, *pieces, *([pinned(weights)] * count), tap_table)
    if not direct:
        product = product.reshape(rows, blocks, chan).transpose(1, 0, 2)
    return query, product


def transform_into(fwd_ref, in_ref, picks, out_ref, places):
    block, chan = in_ref.shape[1:]
    group = 2 if chan % 128 == 0 and len(picks) % 2 == 0 else 1
    for start in range(0, len(picks), group):
        signal = jnp.concatenate([in_ref[k] for k in picks[start : start + group]], 1)
        stacked = jnp.concatenate([signal, signal], 0)
        result = jnp.dot(fwd_ref[...], stacked, preferred_element_type=f32)
        for j in range(group):
            lanes = slice(j * chan, (j + 1) * chan)
            out_ref[0, places[start + j]] = result[:block, lanes]
            out_ref[1, places[start + j]] = result[block:, lanes]


def filter_kernel(fwd_ref, sign_ref, taps_ref, out_hbm, out_ref, spec_ref, sem):
    count, block, chan = taps_ref.shape
    transform_into(fwd_ref, taps_ref, range(count), spec_ref, range(count))
    sign = sign_ref[:, :chan]

    def body(i, carry):
        rows = pl.ds(pl.multiple_of(i * 8, 8), 8)
        prev = None
        for k in range(count):
            real, imag = spec_ref[0, k, rows, :], spec_ref[1, k, rows, :]
            if prev is None:
                out_ref[k % 2, 0, k // 2, rows, :] = real
                out_ref[k % 2, 1, k // 2, rows, :] = imag
            else:
                out_ref[k % 2, 0, k // 2, rows, :] = real - sign * prev[1]
                out_ref[k % 2, 1, k // 2, rows, :] = imag + sign * prev[0]
            prev = (real, imag)
        return carry

    lax.fori_loop(0, block // 8, body, 0)
    copy = pltpu.make_async_copy(out_ref, out_hbm, sem)
    copy.start()
    copy.wait()


def filter_spectra(fwd, sign, taps):
    count, block, chan = taps.shape
    shape = (2, 2, count // 2, block, chan)
    return pl.pallas_call(
        filter_kernel,
        in_specs=[vmem_spec()] * 3,
        out_specs=hbm_spec(),
        out_shape=pltpu.HBM(shape, f32),
        scratch_shapes=[
            pltpu.VMEM(shape, f32),
            pltpu.VMEM((2, count, block, chan), f32),
            pltpu.SemaphoreType.DMA,
        ],
        compiler_params=params(16),
        cost_estimate=cost(2 * 2 * count * chan * 4 * block * block, 8 * count * block * chan),
        name="filter_spectra",
    )(fwd, sign, taps)


def accumulate(filt_ref, spec_ref, ahead, init_ref, write):
    half, block, chan = spec_ref.shape[1:]

    def body(i, carry):
        rows = pl.ds(pl.multiple_of(i * 8, 8), 8)
        for target in range(half):
            real = imag = None
            if init_ref is not None:
                real, imag = init_ref[0, target, rows, :], init_ref[1, target, rows, :]
            for source in range(target - ahead + 1):
                lag = target - ahead - source
                xr, xi = spec_ref[0, source, rows, :], spec_ref[1, source, rows, :]
                gr, gi = filt_ref[0, lag, rows, :], filt_ref[1, lag, rows, :]
                if real is None:
                    real, imag = xr * gr - xi * gi, xr * gi + xi * gr
                else:
                    real = real + xr * gr - xi * gi
                    imag = imag + xr * gi + xi * gr
            if real is None:
                real = imag = jnp.zeros((8, chan), f32)
            write(rows, target, real, imag)
        return carry

    lax.fori_loop(0, block // 8, body, 0)


def inverse_block(bwd_ref, sum_ref, out_ref, start):
    chan = sum_ref.shape[2]
    group = inverse_group(sum_ref)
    full = jnp.concatenate([sum_ref[start + j] for j in range(group)], 1)
    high = full.astype(bf16)
    low = (full - high.astype(f32)).astype(bf16)
    stacked = jnp.concatenate([high, high, low], 0)
    result = jnp.dot(bwd_ref[...], stacked, preferred_element_type=f32).astype(out_ref.dtype)
    for j in range(group):
        out_ref[start + j] = result[:, j * chan : (j + 1) * chan]


def inverse_group(sum_ref):
    count, _, chan = sum_ref.shape
    return 2 if chan % 128 == 0 and count % 2 == 0 else 1


def inverse_out(bwd_ref, sum_ref, out_ref, out_hbm, sems):
    count = sum_ref.shape[0]
    group = inverse_group(sum_ref)
    copies = []
    for start in range(0, count, group):
        inverse_block(bwd_ref, sum_ref, out_ref, start)
        here = slice(start, start + group)
        copies.append(pltpu.make_async_copy(out_ref.at[here], out_hbm.at[here], sems.at[start // group]))
        copies[-1].start()
    return copies


def write_sums(sum_ref, block):
    def write(rows, place, real, imag):
        sum_ref[place, rows, :] = real
        sum_ref[place, pl.ds(rows.start + block, 8), :] = imag

    return write


def write_spec(ref):
    def write(rows, place, real, imag):
        ref[0, place, rows, :] = real
        ref[1, place, rows, :] = imag

    return write


def early_kernel(fwd_ref, filt_hbm, half_ref, same_hbm, other_hbm, filt_ref, spec_ref, same_ref, other_ref, sems):
    half = half_ref.shape[0]
    load = pltpu.make_async_copy(filt_hbm, filt_ref, sems.at[0])
    load.start()
    transform_into(fwd_ref, half_ref, range(half), spec_ref, range(half))
    load.wait()
    accumulate(filt_ref.at[0], spec_ref, 0, None, write_spec(same_ref))
    same_out = pltpu.make_async_copy(same_ref, same_hbm, sems.at[1])
    same_out.start()
    accumulate(filt_ref.at[1], spec_ref, 1, None, write_spec(other_ref))
    other_out = pltpu.make_async_copy(other_ref, other_hbm, sems.at[2])
    other_out.start()
    same_out.wait()
    other_out.wait()


def middle_kernel(
    fwd_ref, bwd_ref, filt_hbm, half_ref, init_hbm, out_hbm, spec_hbm,
    filt_ref, init_ref, spec_ref, sum_ref, out_ref, sems, out_sems,
):
    half, block, _ = half_ref.shape
    load_filt = pltpu.make_async_copy(filt_hbm.at[0], filt_ref, sems.at[0])
    load_init = pltpu.make_async_copy(init_hbm, init_ref, sems.at[1])
    load_filt.start()
    load_init.start()
    transform_into(fwd_ref, half_ref, range(half), spec_ref, range(half))
    keep_spec = pltpu.make_async_copy(spec_ref, spec_hbm, sems.at[2])
    keep_spec.start()
    load_filt.wait()
    load_init.wait()
    accumulate(filt_ref, spec_ref, 0, init_ref, write_sums(sum_ref, block))
    copies = inverse_out(bwd_ref, sum_ref, out_ref, out_hbm, out_sems)
    keep_spec.wait()
    for copy in copies:
        copy.wait()


def late_kernel(
    bwd_ref, filt_hbm, spec_hbm, init_hbm, out_hbm,
    filt_ref, spec_ref, init_ref, sum_ref, out_ref, sems, out_sems,
):
    block = spec_ref.shape[2]
    loads = [
        pltpu.make_async_copy(filt_hbm.at[1], filt_ref, sems.at[0]),
        pltpu.make_async_copy(spec_hbm, spec_ref, sems.at[1]),
        pltpu.make_async_copy(init_hbm, init_ref, sems.at[2]),
    ]
    for load in loads:
        load.start()
    for load in loads:
        load.wait()
    accumulate(filt_ref, spec_ref, 0, init_ref, write_sums(sum_ref, block))
    for copy in inverse_out(bwd_ref, sum_ref, out_ref, out_hbm, out_sems):
        copy.wait()


def early(fwd, filt, part):
    half, block, chan = part.shape
    spec = pltpu.HBM((2, half, block, chan), f32)
    return pl.pallas_call(
        early_kernel,
        in_specs=[vmem_spec(), hbm_spec(), vmem_spec()],
        out_specs=[hbm_spec()] * 2,
        out_shape=[spec, spec],
        scratch_shapes=[pltpu.VMEM(filt.shape, f32)]
        + [pltpu.VMEM(spec.shape, f32)] * 3
        + [pltpu.SemaphoreType.DMA((3,))],
        compiler_params=params(32),
        cost_estimate=cost(2 * half * chan * 4 * block * block * 2, 32 * half * block * chan),
        name="early_blocks",
    )(fwd, pinned(filt), part)


def middle(fwd, bwd, filt, part, init):
    half, block, chan = part.shape
    spec = (2, half, block, chan)
    return pl.pallas_call(
        middle_kernel,
        in_specs=[vmem_spec(), vmem_spec(), hbm_spec(), vmem_spec(), hbm_spec()],
        out_specs=[hbm_spec()] * 2,
        out_shape=[pltpu.HBM(part.shape, bf16), pltpu.HBM(spec, f32)],
        scratch_shapes=[pltpu.VMEM(spec, f32)] * 3
        + [pltpu.VMEM((half, 2 * block, chan), f32), pltpu.VMEM(part.shape, bf16)]
        + [pltpu.SemaphoreType.DMA((3,)), pltpu.SemaphoreType.DMA((half,))],
        compiler_params=params(32),
        cost_estimate=cost(2 * half * chan * 10 * block * block * 2, 32 * half * block * chan),
        name="middle_blocks",
    )(fwd, bwd, pinned(filt), part, pinned(init))


def late(bwd, filt, spec, init):
    _, half, block, chan = spec.shape
    return pl.pallas_call(
        late_kernel,
        in_specs=[vmem_spec()] + [hbm_spec()] * 3,
        out_specs=hbm_spec(),
        out_shape=pltpu.HBM((half, block, chan), bf16),
        scratch_shapes=[pltpu.VMEM(spec.shape, f32)] * 3
        + [pltpu.VMEM((half, 2 * block, chan), f32), pltpu.VMEM((half, block, chan), bf16)]
        + [pltpu.SemaphoreType.DMA((3,)), pltpu.SemaphoreType.DMA((half,))],
        compiler_params=params(32),
        cost_estimate=cost(2 * half * chan * 6 * block * block * 2, 32 * half * block * chan),
        name="late_blocks",
    )(bwd, pinned(filt), pinned(spec), pinned(init))


def output_kernel(picks, own_ref, query_ref, conv_ref, w_hbm, *refs):
    count = len(picks)
    out_refs = refs[:count]
    gated_ref, w_ref, sems = refs[count:]
    blocks, _, chan = conv_ref.shape
    wide = out_refs[0].shape[1]
    tile = 512

    def load(slot, col):
        base = (own_ref[0] ^ picks[slot]) * wide + col
        cols = pl.ds(pl.multiple_of(base, tile), tile)
        return pltpu.make_async_copy(w_hbm.at[:, cols], w_ref.at[slot, :, col : col + tile], sems.at[slot, col // tile])

    places = [(slot, col) for slot in range(count) for col in range(0, wide, tile)]
    for place in places:
        load(*place).start()
    for k in range(blocks):
        lanes = slice(k * chan, (k + 1) * chan)
        gated_ref[:, lanes] = (query_ref[:, lanes].astype(f32) * conv_ref[k].astype(f32)).astype(bf16)
    for slot, col in places:
        load(slot, col).wait()
        w = w_ref[slot, :, col : col + tile]
        out_refs[slot][:, col : col + tile] = jnp.dot(gated_ref[...], w, preferred_element_type=f32).astype(bf16)


def output_terms(own, query, conv, weights, parts, picks):
    rows, width = query.shape
    wide = weights.shape[1] // parts
    terms = pl.pallas_call(
        lambda *refs: output_kernel(picks, *refs),
        grid_spec=pltpu.PrefetchScalarGridSpec(
            num_scalar_prefetch=1,
            grid=(),
            in_specs=[vmem_spec()] * 2 + [hbm_spec()],
            out_specs=[vmem_spec()] * len(picks),
            scratch_shapes=[
                pltpu.VMEM((rows, width), bf16),
                pltpu.VMEM((len(picks), width, wide), bf16),
                pltpu.SemaphoreType.DMA((len(picks), wide // 512)),
            ],
        ),
        out_shape=[jax.ShapeDtypeStruct((rows, wide), bf16)] * len(picks),
        compiler_params=params(16),
        cost_estimate=cost(2 * rows * width * len(picks) * wide, 2 * width * len(picks) * wide),
        name="output_terms",
    )(own, query, conv, pinned(weights))
    return dict(zip(picks, terms))


def body(sequence, in_weight, short_weight, filter_taps, out_weight):
    rows, width = sequence.shape
    blocks = lax.axis_size("seq")
    parts = lax.axis_size("ch")
    chan = width // blocks
    block = rows // 2
    fwd, bwd, sign = fourier_tables(block)
    own = lax.axis_index("ch").astype(jnp.int32).reshape(1)
    weights = in_weight.transpose(1, 0, 2)
    tap_table = short_weight.astype(f32).transpose(1, 0, 2)
    bits = [1 << k for k in range(parts.bit_length() - 1)]

    def exchange(values):
        return lax.all_to_all(values, "seq", split_axis=0, concat_axis=0, tiled=True)

    rows_odd = lax.optimization_barrier(sequence[block - HALO :])
    border = lax.ppermute(rows_odd[block:], "seq", [(i, i + 1) for i in range(blocks - 1)])
    filter_taps, border = lax.optimization_barrier((filter_taps, border))
    taps = exchange(filter_taps.reshape(rows, blocks, chan).transpose(1, 0, 2))

    def gather_far(shard):
        pieces = {0: shard}
        for bit in bits[1:]:
            pieces.update({p | bit: swap(piece, "ch", bit) for p, piece in pieces.items()})
        return pieces

    def gather_near(pieces):
        pieces = dict(pieces)
        for bit in bits[:1]:
            pieces.update({p | bit: swap(piece, "ch", bit) for p, piece in pieces.items()})
        return [pieces[p] for p in range(parts)]

    rows_even = jnp.concatenate([border, sequence[:block]], 0)
    far_odd = gather_far(rows_odd)
    rows_even, far_odd = lax.optimization_barrier((rows_even, far_odd))
    far_even = gather_far(rows_even)
    query_odd, product_odd = project(own, gather_near(far_odd), weights, tap_table, blocks)
    product_odd, far_even = lax.optimization_barrier((product_odd, far_even))
    product_odd = exchange(product_odd)
    query_even, product_even = project(own, gather_near(far_even), weights, tap_table, blocks)
    product_even = exchange(product_even)
    filt = filter_spectra(fwd, sign, taps.reshape(2 * blocks, block, chan))
    init_odd, init_even = early(fwd, filt, product_odd)
    conv_even, spec_even = middle(fwd, bwd, filt, product_even, init_even)
    conv_even = exchange(conv_even)
    conv_odd = late(bwd, filt, spec_even, init_odd)
    conv_even, conv_odd = lax.optimization_barrier((conv_even, conv_odd))
    conv_odd = exchange(conv_odd)

    def reduce(held, picked):
        for bit in picked:
            arrived = {p ^ bit: swap(held[p], "ch", bit) for p in held if p & bit}
            held = {p: (held[p].astype(f32) + arrived[p].astype(f32)).astype(bf16) for p in arrived}
        return held

    far, near = list(range(2, parts)), list(range(2))

    def far_sums(query, conv):
        return reduce(output_terms(own, query, conv, out_weight, parts, far), bits[:1])

    def near_sums(query, conv):
        return reduce(output_terms(own, query, conv, out_weight, parts, near), bits[:1])

    far_even = far_sums(query_even, conv_even)
    near_even = near_sums(query_even, conv_even)
    result_even = reduce({**far_even, **near_even}, bits[1:])[0]
    conv_odd, result_even = lax.optimization_barrier((conv_odd, result_even))
    far_odd = far_sums(query_odd, conv_odd)
    near_odd = near_sums(query_odd, conv_odd)
    result_odd = reduce({**far_odd, **near_odd}, bits[1:])[0]
    return jnp.concatenate([result_even, result_odd], 0)


def solution(mesh):
    return jax.shard_map(
        body,
        mesh=mesh,
        in_specs=(
            P("seq", "ch"),
            P(None, None, "ch"),
            P(None, None, "ch"),
            P("seq", "ch"),
            P("ch", None),
        ),
        out_specs=P("seq", "ch"),
        check_vma=False,
    )
```

```python
import math

import jax
import jax.numpy as jnp
import numpy as np
from jax import lax
from jax.experimental import pallas as pl
from jax.experimental.pallas import tpu as pltpu
from jax.sharding import PartitionSpec as P

TAPS = 7
HALO = 16
AHEAD = 3
bf16 = jnp.bfloat16
f32 = jnp.float32


def split_parts(table):
    high = table.astype(bf16)
    low = (table - high.astype(np.float64)).astype(bf16)
    return high, low


def fourier_tables(block):
    freqs = np.arange(block)[:, None] + 0.5
    spots = np.arange(block)[None, :]
    angle = 2.0 * math.pi * freqs * spots / (2 * block)
    forward = np.concatenate([np.cos(angle), -np.sin(angle)], 0)
    backward = np.concatenate([np.cos(angle).T, -np.sin(angle).T], 1) / block
    fwd_high, fwd_low = split_parts(forward)
    bwd_high, bwd_low = split_parts(backward)
    fwd = np.concatenate([fwd_high, fwd_low], 1)
    bwd = np.concatenate([bwd_high, bwd_low, bwd_high], 1)
    sign = np.broadcast_to(np.where(np.arange(8) % 2 == 0, 1.0, -1.0)[:, None], (8, 128))
    return fwd, bwd, sign.astype(np.float32)


def swap(shard, axis, bit):
    size = lax.axis_size(axis)
    return lax.ppermute(shard, axis, [(i, i ^ bit) for i in range(size)])


def vmem_spec():
    return pl.BlockSpec(memory_space=pltpu.VMEM)


def hbm_spec():
    return pl.BlockSpec(memory_space=pltpu.HBM)


def pinned(array):
    return pltpu.with_memory_space_constraint(array, pltpu.HBM)


def params(mib):
    return pltpu.CompilerParams(vmem_limit_bytes=mib * 1024 * 1024)


def cost(flops, moved):
    return pl.CostEstimate(flops=flops, bytes_accessed=moved, transcendentals=0)


def project_kernel(pieces, strip, own_ref, *refs):
    x_refs = refs[:pieces]
    w_refs = refs[pieces : 2 * pieces]
    tap_ref, query_ref, product_ref, ext_ref = refs[2 * pieces :]
    rows, width = query_ref.shape
    for branch in range(3):
        total = None
        for x_ref, w_ref in zip(x_refs, w_refs):
            term = jnp.dot(x_ref[...], w_ref[branch], preferred_element_type=f32)
            total = term if total is None else total + term
        ext_ref[branch] = total.astype(bf16).astype(f32)
    step = 64
    for lane in range(0, width, strip):
        lanes = slice(lane, lane + strip)
        for row in range(0, rows, step):

            def mixed(branch):
                running = None
                for offset in range(TAPS):
                    lead = row + HALO - offset
                    term = tap_ref[branch, offset : offset + 1, lanes] * ext_ref[branch, lead : lead + step, lanes]
                    running = term if running is None else running + term
                return running.astype(bf16)

            here = slice(row, row + step)
            query_ref[here, lanes] = mixed(0)
            product = (mixed(1).astype(f32) * mixed(2).astype(f32)).astype(bf16)
            if len(product_ref.shape) == 3:
                product_ref[lane // strip, here, :] = product
            else:
                product_ref[here, lanes] = product


def project(own, pieces, weights, tap_table, blocks):
    count = len(pieces)
    rows_in, depth = pieces[0].shape
    rows = rows_in - HALO
    width = weights.shape[2]
    tile = 256
    chan = width // blocks
    direct = chan % 128 == 0 and tile % chan == 0
    strip = chan if direct else 128
    if direct:
        product_shape = (blocks, rows, chan)
        product_spec = pl.BlockSpec((tile // chan, rows, chan), lambda i, own: (i, 0, 0))
    else:
        product_shape = (rows, width)
        product_spec = pl.BlockSpec((rows, tile), lambda i, own: (0, i))

    def weight_spec(p):
        return pl.BlockSpec((3, depth, tile), lambda i, own: (0, own[0] ^ p, i))

    query, product = pl.pallas_call(
        lambda *refs: project_kernel(count, strip, *refs),
        grid_spec=pltpu.PrefetchScalarGridSpec(
            num_scalar_prefetch=1,
            grid=(width // tile,),
            in_specs=[vmem_spec()] * count
            + [weight_spec(p) for p in range(count)]
            + [pl.BlockSpec((3, TAPS, tile), lambda i, own: (0, 0, i))],
            out_specs=[pl.BlockSpec((rows, tile), lambda i, own: (0, i)), product_spec],
            scratch_shapes=[pltpu.VMEM((3, rows_in, tile), f32)],
        ),
        out_shape=[pltpu.HBM((rows, width), bf16), pltpu.HBM(product_shape, bf16)],
        compiler_params=params(20),
        cost_estimate=cost(2 * rows_in * count * depth * 3 * width, 6 * count * depth * width),
        name="project",
    )(own, *pieces, *([pinned(weights)] * count), tap_table)
    if not direct:
        product = product.reshape(rows, blocks, chan).transpose(1, 0, 2)
    return query, product


def transform_into(fwd_ref, in_ref, picks, out_ref, places):
    block, chan = in_ref.shape[1:]
    group = 2 if chan % 128 == 0 and len(picks) % 2 == 0 else 1
    for start in range(0, len(picks), group):
        signal = jnp.concatenate([in_ref[k] for k in picks[start : start + group]], 1)
        stacked = jnp.concatenate([signal, signal], 0)
        result = jnp.dot(fwd_ref[...], stacked, preferred_element_type=f32)
        for j in range(group):
            lanes = slice(j * chan, (j + 1) * chan)
            out_ref[0, places[start + j]] = result[:block, lanes]
            out_ref[1, places[start + j]] = result[block:, lanes]


def filter_kernel(fwd_ref, sign_ref, taps_ref, out_hbm, out_ref, spec_ref, sem):
    count, block, chan = taps_ref.shape
    transform_into(fwd_ref, taps_ref, range(count), spec_ref, range(count))
    sign = sign_ref[:, :chan]

    def body(i, carry):
        rows = pl.ds(pl.multiple_of(i * 8, 8), 8)
        prev = None
        for k in range(count):
            real, imag = spec_ref[0, k, rows, :], spec_ref[1, k, rows, :]
            if prev is None:
                out_ref[k % 2, 0, k // 2, rows, :] = real
                out_ref[k % 2, 1, k // 2, rows, :] = imag
            else:
                out_ref[k % 2, 0, k // 2, rows, :] = real - sign * prev[1]
                out_ref[k % 2, 1, k // 2, rows, :] = imag + sign * prev[0]
            prev = (real, imag)
        return carry

    lax.fori_loop(0, block // 8, body, 0)
    copy = pltpu.make_async_copy(out_ref, out_hbm, sem)
    copy.start()
    copy.wait()


def filter_spectra(fwd, sign, taps):
    count, block, chan = taps.shape
    shape = (2, 2, count // 2, block, chan)
    return pl.pallas_call(
        filter_kernel,
        in_specs=[vmem_spec()] * 3,
        out_specs=hbm_spec(),
        out_shape=pltpu.HBM(shape, f32),
        scratch_shapes=[
            pltpu.VMEM(shape, f32),
            pltpu.VMEM((2, count, block, chan), f32),
            pltpu.SemaphoreType.DMA,
        ],
        compiler_params=params(16),
        cost_estimate=cost(2 * 2 * count * chan * 4 * block * block, 8 * count * block * chan),
        name="filter_spectra",
    )(fwd, sign, taps)


def accumulate(filt_ref, spec_ref, ahead, init_ref, write, begin=0, end=None):
    half, block, chan = spec_ref.shape[1:]

    def body(i, carry):
        rows = pl.ds(pl.multiple_of(i * 8, 8), 8)
        for target in range(half):
            real = imag = None
            if init_ref is not None:
                real, imag = init_ref[0, target, rows, :], init_ref[1, target, rows, :]
            for source in range(target - ahead + 1):
                lag = target - ahead - source
                xr, xi = spec_ref[0, source, rows, :], spec_ref[1, source, rows, :]
                gr, gi = filt_ref[0, lag, rows, :], filt_ref[1, lag, rows, :]
                if real is None:
                    real, imag = xr * gr - xi * gi, xr * gi + xi * gr
                else:
                    real = real + xr * gr - xi * gi
                    imag = imag + xr * gi + xi * gr
            if real is None:
                real = imag = jnp.zeros((8, chan), f32)
            write(rows, target, real, imag)
        return carry

    lax.fori_loop(begin // 8, (block if end is None else end) // 8, body, 0)


def inverse_block(bwd_ref, sum_ref, out_ref, start):
    chan = sum_ref.shape[2]
    group = inverse_group(sum_ref)
    full = jnp.concatenate([sum_ref[start + j] for j in range(group)], 1)
    high = full.astype(bf16)
    low = (full - high.astype(f32)).astype(bf16)
    stacked = jnp.concatenate([high, high, low], 0)
    result = jnp.dot(bwd_ref[...], stacked, preferred_element_type=f32).astype(out_ref.dtype)
    for j in range(group):
        out_ref[start + j] = result[:, j * chan : (j + 1) * chan]


def inverse_group(sum_ref):
    count, _, chan = sum_ref.shape
    return 2 if chan % 128 == 0 and count % 2 == 0 else 1


def inverse_out(bwd_ref, sum_ref, out_ref, out_hbm, sems):
    count = sum_ref.shape[0]
    group = inverse_group(sum_ref)
    copies = []
    for start in range(0, count, group):
        inverse_block(bwd_ref, sum_ref, out_ref, start)
        here = slice(start, start + group)
        copies.append(pltpu.make_async_copy(out_ref.at[here], out_hbm.at[here], sems.at[start // group]))
        copies[-1].start()
    return copies


def write_sums(sum_ref, block):
    def write(rows, place, real, imag):
        sum_ref[place, rows, :] = real
        sum_ref[place, pl.ds(rows.start + block, 8), :] = imag

    return write


def write_spec(ref):
    def write(rows, place, real, imag):
        ref[0, place, rows, :] = real
        ref[1, place, rows, :] = imag

    return write


def early_kernel(fwd_ref, filt_hbm, half_ref, same_hbm, other_hbm, filt_ref, spec_ref, same_ref, other_ref, sems):
    half = half_ref.shape[0]
    load = pltpu.make_async_copy(filt_hbm, filt_ref, sems.at[0])
    load.start()
    transform_into(fwd_ref, half_ref, range(half), spec_ref, range(half))
    load.wait()
    accumulate(filt_ref.at[0], spec_ref, 0, None, write_spec(same_ref))
    same_out = pltpu.make_async_copy(same_ref, same_hbm, sems.at[1])
    same_out.start()
    accumulate(filt_ref.at[1], spec_ref, 1, None, write_spec(other_ref))
    other_out = pltpu.make_async_copy(other_ref, other_hbm, sems.at[2])
    other_out.start()
    same_out.wait()
    other_out.wait()


def middle_kernel(
    fwd_ref, bwd_ref, filt_hbm, half_ref, init_hbm, out_hbm, spec_hbm,
    filt_ref, init_ref, spec_ref, sum_ref, out_ref, sems, out_sems,
):
    half, block, _ = half_ref.shape
    cut = block // 4
    loads = []
    for k in range(4):
        rows = pl.ds(k * cut, cut)
        loads.append(pltpu.make_async_copy(filt_hbm.at[0, :, :, rows], filt_ref.at[:, :, rows], sems.at[2 * k]))
        loads.append(pltpu.make_async_copy(init_hbm.at[:, :, rows], init_ref.at[:, :, rows], sems.at[2 * k + 1]))
    for load in loads:
        load.start()
    transform_into(fwd_ref, half_ref, range(half), spec_ref, range(half))
    for k in range(4):
        loads[2 * k].wait()
        loads[2 * k + 1].wait()
        accumulate(filt_ref, spec_ref, 0, init_ref, write_sums(sum_ref, block), k * cut, (k + 1) * cut)
    keep_spec = pltpu.make_async_copy(spec_ref, spec_hbm, sems.at[8])
    keep_spec.start()
    copies = inverse_out(bwd_ref, sum_ref, out_ref, out_hbm, out_sems)
    keep_spec.wait()
    for copy in copies:
        copy.wait()


def late_kernel(
    bwd_ref, filt_hbm, spec_hbm, init_hbm, out_hbm,
    filt_ref, spec_ref, init_ref, sum_ref, out_ref, sems, out_sems,
):
    block = spec_ref.shape[2]
    loads = [
        pltpu.make_async_copy(filt_hbm.at[1], filt_ref, sems.at[0]),
        pltpu.make_async_copy(spec_hbm, spec_ref, sems.at[1]),
        pltpu.make_async_copy(init_hbm, init_ref, sems.at[2]),
    ]
    for load in loads:
        load.start()
    for load in loads:
        load.wait()
    accumulate(filt_ref, spec_ref, 0, init_ref, write_sums(sum_ref, block))
    for copy in inverse_out(bwd_ref, sum_ref, out_ref, out_hbm, out_sems):
        copy.wait()


def early(fwd, filt, part):
    half, block, chan = part.shape
    spec = pltpu.HBM((2, half, block, chan), f32)
    return pl.pallas_call(
        early_kernel,
        in_specs=[vmem_spec(), hbm_spec(), vmem_spec()],
        out_specs=[hbm_spec()] * 2,
        out_shape=[spec, spec],
        scratch_shapes=[pltpu.VMEM(filt.shape, f32)]
        + [pltpu.VMEM(spec.shape, f32)] * 3
        + [pltpu.SemaphoreType.DMA((3,))],
        compiler_params=params(32),
        cost_estimate=cost(2 * half * chan * 4 * block * block * 2, 32 * half * block * chan),
        name="early_blocks",
    )(fwd, pinned(filt), part)


def middle(fwd, bwd, filt, part, init):
    half, block, chan = part.shape
    spec = (2, half, block, chan)
    return pl.pallas_call(
        middle_kernel,
        in_specs=[vmem_spec(), vmem_spec(), hbm_spec(), vmem_spec(), hbm_spec()],
        out_specs=[hbm_spec()] * 2,
        out_shape=[pltpu.HBM(part.shape, bf16), pltpu.HBM(spec, f32)],
        scratch_shapes=[pltpu.VMEM(spec, f32)] * 3
        + [pltpu.VMEM((half, 2 * block, chan), f32), pltpu.VMEM(part.shape, bf16)]
        + [pltpu.SemaphoreType.DMA((9,)), pltpu.SemaphoreType.DMA((half,))],
        compiler_params=params(32),
        cost_estimate=cost(2 * half * chan * 10 * block * block * 2, 32 * half * block * chan),
        name="middle_blocks",
    )(fwd, bwd, pinned(filt), part, pinned(init))


def late(bwd, filt, spec, init):
    _, half, block, chan = spec.shape
    return pl.pallas_call(
        late_kernel,
        in_specs=[vmem_spec()] + [hbm_spec()] * 3,
        out_specs=hbm_spec(),
        out_shape=pltpu.HBM((half, block, chan), bf16),
        scratch_shapes=[pltpu.VMEM(spec.shape, f32)] * 3
        + [pltpu.VMEM((half, 2 * block, chan), f32), pltpu.VMEM((half, block, chan), bf16)]
        + [pltpu.SemaphoreType.DMA((3,)), pltpu.SemaphoreType.DMA((half,))],
        compiler_params=params(32),
        cost_estimate=cost(2 * half * chan * 6 * block * block * 2, 32 * half * block * chan),
        name="late_blocks",
    )(bwd, pinned(filt), pinned(spec), pinned(init))


def output_kernel(picks, own_ref, query_ref, conv_ref, w_hbm, *refs):
    count = len(picks)
    out_refs = refs[:count]
    gated_ref, w_ref, sems = refs[count:]
    blocks, _, chan = conv_ref.shape
    wide = out_refs[0].shape[1]
    tile = 512

    def load(slot, col):
        base = (own_ref[0] ^ picks[slot]) * wide + col
        cols = pl.ds(pl.multiple_of(base, tile), tile)
        return pltpu.make_async_copy(w_hbm.at[:, cols], w_ref.at[slot, :, col : col + tile], sems.at[slot, col // tile])

    places = [(slot, col) for slot in range(count) for col in range(0, wide, tile)]
    for place in places[:AHEAD]:
        load(*place).start()
    for k in range(blocks):
        lanes = slice(k * chan, (k + 1) * chan)
        gated_ref[:, lanes] = (query_ref[:, lanes].astype(f32) * conv_ref[k].astype(f32)).astype(bf16)
    for step, (slot, col) in enumerate(places):
        load(slot, col).wait()
        for place in places[step + AHEAD :][:1]:
            load(*place).start()
        w = w_ref[slot, :, col : col + tile]
        out_refs[slot][:, col : col + tile] = jnp.dot(gated_ref[...], w, preferred_element_type=f32).astype(bf16)


def output_terms(own, query, conv, weights, parts, picks):
    rows, width = query.shape
    wide = weights.shape[1] // parts
    terms = pl.pallas_call(
        lambda *refs: output_kernel(picks, *refs),
        grid_spec=pltpu.PrefetchScalarGridSpec(
            num_scalar_prefetch=1,
            grid=(),
            in_specs=[vmem_spec()] * 2 + [hbm_spec()],
            out_specs=[vmem_spec()] * len(picks),
            scratch_shapes=[
                pltpu.VMEM((rows, width), bf16),
                pltpu.VMEM((len(picks), width, wide), bf16),
                pltpu.SemaphoreType.DMA((len(picks), wide // 512)),
            ],
        ),
        out_shape=[jax.ShapeDtypeStruct((rows, wide), bf16)] * len(picks),
        compiler_params=params(20),
        cost_estimate=cost(2 * rows * width * len(picks) * wide, 2 * width * len(picks) * wide),
        name="output_terms",
    )(own, query, conv, pinned(weights))
    return dict(zip(picks, terms))


def body(sequence, in_weight, short_weight, filter_taps, out_weight):
    rows, width = sequence.shape
    blocks = lax.axis_size("seq")
    parts = lax.axis_size("ch")
    chan = width // blocks
    block = rows // 2
    fwd, bwd, sign = fourier_tables(block)
    own = lax.axis_index("ch").astype(jnp.int32).reshape(1)
    weights = in_weight.transpose(1, 0, 2)
    tap_table = short_weight.astype(f32).transpose(1, 0, 2)
    bits = [1 << k for k in range(parts.bit_length() - 1)]

    def exchange(values):
        return lax.all_to_all(values, "seq", split_axis=0, concat_axis=0, tiled=True)

    rows_odd = lax.optimization_barrier(sequence[block - HALO :])
    border = lax.ppermute(rows_odd[block:], "seq", [(i, i + 1) for i in range(blocks - 1)])
    filter_taps, border = lax.optimization_barrier((filter_taps, border))
    taps = exchange(filter_taps.reshape(rows, blocks, chan).transpose(1, 0, 2))

    def gather_far(shard):
        pieces = {0: shard}
        for bit in bits[1:]:
            pieces.update({p | bit: swap(piece, "ch", bit) for p, piece in pieces.items()})
        return pieces

    def gather_near(pieces):
        pieces = dict(pieces)
        for bit in bits[:1]:
            pieces.update({p | bit: swap(piece, "ch", bit) for p, piece in pieces.items()})
        return [pieces[p] for p in range(parts)]

    rows_even = jnp.concatenate([border, sequence[:block]], 0)
    far_odd = gather_far(rows_odd)
    rows_even, far_odd = lax.optimization_barrier((rows_even, far_odd))
    far_even = gather_far(rows_even)
    query_odd, product_odd = project(own, gather_near(far_odd), weights, tap_table, blocks)
    product_odd, far_even = lax.optimization_barrier((product_odd, far_even))
    product_odd = exchange(product_odd)
    query_even, product_even = project(own, gather_near(far_even), weights, tap_table, blocks)
    product_even = exchange(product_even)
    filt = filter_spectra(fwd, sign, taps.reshape(2 * blocks, block, chan))
    init_odd, init_even = early(fwd, filt, product_odd)
    conv_even, spec_even = middle(fwd, bwd, filt, product_even, init_even)
    conv_even = exchange(conv_even)
    conv_odd = late(bwd, filt, spec_even, init_odd)
    conv_even, conv_odd = lax.optimization_barrier((conv_even, conv_odd))
    conv_odd = exchange(conv_odd)

    def reduce(held, picked):
        for bit in picked:
            arrived = {p ^ bit: swap(held[p], "ch", bit) for p in held if p & bit}
            held = {p: (held[p].astype(f32) + arrived[p].astype(f32)).astype(bf16) for p in arrived}
        return held

    everyone = list(range(parts))
    terms_even = output_terms(own, query_even, conv_even, out_weight, parts, everyone)
    result_even = reduce(terms_even, bits)[0]
    terms_odd = output_terms(own, query_odd, conv_odd, out_weight, parts, everyone)
    sums_odd = reduce(terms_odd, bits[:1])
    result_even, sums_odd = lax.optimization_barrier((result_even, sums_odd))
    return jnp.concatenate([result_even, reduce(sums_odd, bits[1:])[0]], 0)


def solution(mesh):
    return jax.shard_map(
        body,
        mesh=mesh,
        in_specs=(
            P("seq", "ch"),
            P(None, None, "ch"),
            P(None, None, "ch"),
            P("seq", "ch"),
            P("ch", None),
        ),
        out_specs=P("seq", "ch"),
        check_vma=False,
    )
```
